512 devices in a mesh: row: 16 (over z, core), col: 32 (over x, y).
Axes of the slice: x: 4, y: 8, z: 8, core: 2. Of those that a mesh axis runs over, the one named last changes fastest.
Arguments:
- inputs: bfloat16 [2048, 12288], P('row', 'col'), may hold values from -0.26367188 to 0.26367188
- pre_act: bfloat16 [2048, 24576], P('row', 'col'), may hold values from -8 to 8
- grad_act: bfloat16 [2048, 24576], P('row', 'col'), may hold values from -6 to 6
- weight_t: bfloat16 [24576, 12288], P('row', 'col'), may hold values from -0.0390625 to 0.0390625
Outputs:
- grad_inputs: bfloat16 [2048, 12288], P('row', 'col')
- grad_weight: bfloat16 [24576, 12288], P('row', 'col')
The draws below stay inside these ranges and needn't reach their ends.
All inputs are finite; a program needn't handle non-finite values.
Results may differ from the reference program's by a relative error of at most 0.0049.
Values may be sent and summed in bfloat16 or wider, within the bound.
No kernel may reach another device: no remote copies, remote signals or barrier semaphores. Data moves between devices by JAX's collectives and lax.ppermute only.
A program may use at most 64 MiB of HBM per device.

```python
import jax
import jax.numpy as jnp

D = 12288
FF = 24576
TOKENS = 2048


def block_levels(stream_key, extent, cuts, least, high):
    level, own = 1.0, jax.random.fold_in(stream_key, 6)
    for dim, shards_of in cuts:
        draws = jnp.exp(jax.random.uniform(jax.random.fold_in(own, dim), (shards_of,), jnp.float32, least / len(cuts), high / len(cuts)))
        level = level * jnp.repeat(draws, extent[dim] // shards_of).reshape([-1 if axis == dim else 1 for axis in range(len(extent))])
    return level


def scatter_about(own_key, extent, deviation, limit, cuts=(), held_as=jnp.bfloat16):
    loudness = block_levels(own_key, extent, cuts, -0.22, 0.18) if cuts else 1.0
    drawn = jax.random.normal(own_key, extent, jnp.float32) * deviation * loudness
    return jnp.minimum(jnp.maximum(drawn, -limit), limit).astype(held_as)


def setup_inputs(seed: int = 0) -> dict:
    arg_keys = jax.random.split(jax.random.key(seed), 5)
    inputs = scatter_about(arg_keys[0], (TOKENS, D), (2.0 / (TOKENS ** 0.5)), 0.26367188, ((0, 16), (1, 32)))
    pre_act = scatter_about(arg_keys[1], (TOKENS, FF), 1.5, 8.0, ((0, 16), (1, 32)))
    grad_act = scatter_about(arg_keys[2], (TOKENS, FF), 1.0, 6.0, ((0, 16), (1, 32)))
    weight_t = scatter_about(arg_keys[3], (FF, D), FF ** -0.5, 0.0390625, ((0, 16), (1, 32)))
    return dict(inputs=inputs, pre_act=pre_act, grad_act=grad_act, weight_t=weight_t)


def gelu_prime(value):
    inner = 0.7978845608 * (value + 0.044715 * value * value * value)
    tanh_val = jnp.tanh(inner)
    slope = 0.7978845608 * (1.0 + 0.134145 * value * value)
    return 0.5 * (1.0 + tanh_val) + 0.5 * value * (1.0 - tanh_val * tanh_val) * slope


def reference(inputs, pre_act, grad_act, weight_t):
    hidden_grad = (grad_act.astype(jnp.float32) * gelu_prime(pre_act.astype(jnp.float32))).astype(jnp.bfloat16)
    hidden_wide = hidden_grad.astype(jnp.float32)
    grad_inputs = jnp.dot(hidden_wide, weight_t.astype(jnp.float32), preferred_element_type=jnp.float32).astype(jnp.bfloat16)
    grad_weight = jnp.dot(hidden_wide.T, inputs.astype(jnp.float32), preferred_element_type=jnp.float32).astype(jnp.bfloat16)
    return grad_inputs, grad_weight
```

```python
import jax
import jax.numpy as jnp
from jax import lax
from jax.sharding import Mesh, PartitionSpec as P

ROW = ("z", "core")
COL = ("x", "y")
ALL = ROW + COL
CHUNKS = 2


def gelu_prime(value):
    inner = 0.7978845608 * (value + 0.044715 * value * value * value)
    tanh_val = jnp.tanh(inner)
    slope = 0.7978845608 * (1.0 + 0.134145 * value * value)
    return 0.5 * (1.0 + tanh_val) + 0.5 * value * (1.0 - tanh_val * tanh_val) * slope


def to_unit_rows():
    pairs = []
    for row in range(16):
        for col in range(32):
            target = (col // 2) * 32 + (col % 2) * 16 + row
            pairs.append((row * 32 + col, target))
    return pairs


def dot(a, b, dims):
    return lax.dot_general(a, b, (dims, ((), ())), preferred_element_type=jnp.float32)


def on_device(inputs, pre_act, grad_act, weight_t):
    hidden_grad = (grad_act.astype(jnp.float32) * gelu_prime(pre_act.astype(jnp.float32))).astype(
        jnp.bfloat16
    )
    mine = lax.ppermute(hidden_grad, ALL, to_unit_rows())
    all_inputs = lax.all_gather(inputs, ROW, axis=0)
    size = 128 // CHUNKS
    shares, sums = [], [0.0, 0.0]
    for k in range(CHUNKS):
        block = lax.all_gather(mine[k * size : (k + 1) * size], COL, axis=0)
        halves = [block[h * 16 : (h + 1) * 16].reshape(16 * size, 768) for h in range(2)]
        share = sum(dot(halves[h], weight_t[h * 768 : (h + 1) * 768], ((1,), (0,))) for h in range(2))
        shares.append(lax.psum_scatter(share, ROW, scatter_dimension=0, tiled=True))
        tokens = all_inputs[:, k * size : (k + 1) * size].reshape(16 * size, 384)
        for h in range(2):
            sums[h] = sums[h] + dot(halves[h], tokens, ((0,), (0,)))
    grad_inputs = jnp.concatenate(shares, axis=0).astype(jnp.bfloat16)
    grad_weight = jnp.concatenate([s.astype(jnp.bfloat16) for s in sums], axis=0)
    return (grad_inputs, grad_weight)


def solution(mesh):
    fine = Mesh(mesh.devices.reshape(8, 2, 4, 8), ALL)
    placed = P(ROW, COL)
    return jax.shard_map(
        on_device,
        mesh=fine,
        in_specs=(placed,) * 4,
        out_specs=(placed, placed),
        check_vma=False,
    )
```

```python
import jax
import jax.numpy as jnp
from jax import lax
from jax.sharding import Mesh, PartitionSpec as P

ROW = ("z", "core")
COL = ("x", "y")
ALL = ROW + COL
BF, F32 = jnp.bfloat16, jnp.float32
PART = 32


def gelu_prime(value):
    inner = 0.7978845608 * (value + 0.044715 * value * value * value)
    tanh_val = jnp.tanh(inner)
    slope = 0.7978845608 * (1.0 + 0.134145 * value * value)
    return 0.5 * (1.0 + tanh_val) + 0.5 * value * (1.0 - tanh_val * tanh_val) * slope


def slot_of(row, q):
    z, core = row // 2, row % 2
    x, y = q * 2 + z // 4, core * 4 + z % 4
    return x * 8 + y


def to_slots(swap):
    pairs = []
    for row in range(16):
        for col in range(32):
            q = (col % 2) ^ swap
            pairs.append((row * 32 + col, (col // 2) * 32 + slot_of(row, q)))
    return pairs


def fetch(block, axis, size, step):
    return lax.ppermute(block, axis, [((i + step) % size, i) for i in range(size)])


def dot(a, b, dims):
    return lax.dot_general(a, b, (dims, ((), ())), preferred_element_type=F32)


def place(pieces, at, size):
    first = next(iter(pieces.values()))
    whole = jnp.zeros((size, *first.shape), first.dtype)
    for d, piece in pieces.items():
        start = (lax.rem(at + d + size, size),) + (0,) * first.ndim
        whole = lax.dynamic_update_slice(whole, piece[None], start)
    return whole


def line_of_8(mine, axis, cut):
    got = {0: mine}
    got[1], got[-1] = fetch(mine, axis, 8, 1), fetch(mine, axis, 8, -1)
    got[2], got[-2] = fetch(got[1], axis, 8, 1), fetch(got[-1], axis, 8, -1)
    got[3], got[-3] = fetch(got[2], axis, 8, 1), fetch(got[-2], axis, 8, -1)
    got[4] = jnp.concatenate(
        [fetch(got[2][:cut], axis, 8, 2), fetch(got[-2][cut:], axis, 8, -2)], axis=0
    )
    return got


def line_of_4(mine, axis, cut):
    got = {0: mine}
    got[1], got[-1] = fetch(mine, axis, 4, 1), fetch(mine, axis, 4, -1)
    got[2] = jnp.concatenate(
        [fetch(got[1][:cut], axis, 4, 1), fetch(got[-1][cut:], axis, 4, -1)], axis=0
    )
    return got


def on_device(inputs, pre_act, grad_act, weight_t):
    z, core, x, y = (lax.axis_index(a) for a in ALL)
    hidden = (grad_act.astype(F32) * gelu_prime(pre_act.astype(F32))).astype(BF)
    h = y % 2
    q = x // 2
    same = lax.dynamic_slice_in_dim(hidden, h * 64, 64, 0)
    other = lax.dynamic_slice_in_dim(hidden, (1 - h) * 64, 64, 0)
    same = lax.ppermute(same, ALL, to_slots(0))
    other = lax.ppermute(other, ALL, to_slots(1))
    low = jnp.where(q == 0, same, other)
    high = jnp.where(q == 0, other, same)
    slot = jnp.concatenate([low, high], axis=1)
    part_a, part_b = slot[:PART], slot[PART:]

    all_inputs = lax.all_gather(inputs, ROW, axis=0)
    seen = all_inputs.reshape(2, 4, 2, 2, 2, PART, 384)
    in_a = seen[:, :, :, :, 0].transpose(3, 0, 2, 1, 4, 5).reshape(4, 8 * PART, 384)
    in_b = seen[:, :, :, :, 1].transpose(2, 1, 3, 0, 4, 5).reshape(8, 4 * PART, 384)

    ya = line_of_8(part_a, "y", PART // 2)
    xb = line_of_4(part_b, "x", PART // 2)
    xa = line_of_4(place(ya, y, 8), "x", 4)
    yb = line_of_8(place(xb, x, 4), "y", 2)

    total = 0.0
    share_a, share_b = {}, {}
    for d, block in xa.items():
        flat = block.reshape(8 * PART, 1536)
        share_a[d] = dot(flat, weight_t, ((1,), (0,))).reshape(8, PART, 384)
        tokens = lax.dynamic_index_in_dim(in_a, lax.rem(x + d + 4, 4), 0, False)
        total = total + dot(flat, tokens, ((0,), (0,)))
    for group in ((0, 1, -1), (2, -2), (3, -3, 4)):
        flat = jnp.concatenate([yb[d].reshape(4 * PART, 1536) for d in group], axis=0)
        share = dot(flat, weight_t, ((1,), (0,))).reshape(len(group), 4, PART, 384)
        tokens = []
        for i, d in enumerate(group):
            share_b[d] = share[i]
            tokens.append(lax.dynamic_index_in_dim(in_b, lax.rem(y + d + 8, 8), 0, False))
        total = total + dot(flat, jnp.concatenate(tokens, axis=0), ((0,), (0,)))
    grad_weight = total.astype(BF)

    share_a = place(share_a, x, 4).reshape(2, 2, 2, 4, PART, 384)
    share_b = place(share_b, y, 8).reshape(2, 4, 2, 2, PART, 384).transpose(2, 3, 0, 1, 4, 5)
    share = jnp.stack([share_a, share_b], axis=4)
    keep = lax.dynamic_index_in_dim(share, core, 2, False)
    give = lax.dynamic_index_in_dim(share, 1 - core, 2, False)
    both = keep + lax.ppermute(give, "core", [(0, 1), (1, 0)])
    both = both.transpose(1, 2, 0, 3, 4, 5).reshape(8, 128, 384)
    sums = lax.dynamic_index_in_dim(both, z, 0, False)
    sent = both.astype(BF)
    for d in (4, 3, -3, 2, -2, 1, -1):
        piece = lax.dynamic_index_in_dim(sent, lax.rem(z + d + 8, 8), 0, False)
        sums = sums + fetch(piece, "z", 8, -d).astype(F32)
    return (sums.astype(BF), grad_weight)


def solution(mesh):
    fine = Mesh(mesh.devices.reshape(8, 2, 4, 8), ALL)
    placed = P(ROW, COL)
    return jax.shard_map(
        on_device,
        mesh=fine,
        in_specs=(placed,) * 4,
        out_specs=(placed, placed),
        check_vma=False,
    )
```

```python
import jax
import jax.numpy as jnp
from jax import lax
from jax.sharding import Mesh, PartitionSpec as P

ROW = ("z", "core")
COL = ("x", "y")
ALL = ROW + COL
BF, F32 = jnp.bfloat16, jnp.float32
PART = 32


def gelu_prime(value):
    inner = 0.7978845608 * (value + 0.044715 * value * value * value)
    tanh_val = jnp.tanh(inner)
    slope = 0.7978845608 * (1.0 + 0.134145 * value * value)
    return 0.5 * (1.0 + tanh_val) + 0.5 * value * (1.0 - tanh_val * tanh_val) * slope


def slot_of(row, q):
    z, core = row // 2, row % 2
    x, y = q * 2 + z // 4, core * 4 + z % 4
    return x * 8 + y


def to_slots(swap):
    pairs = []
    for row in range(16):
        for col in range(32):
            q = (col % 2) ^ swap
            pairs.append((row * 32 + col, (col // 2) * 32 + slot_of(row, q)))
    return pairs


def exchange(block, axis, size, turn):
    pairs = []
    for core in range(2):
        for i in range(size):
            step = 1 if (i + core + turn) % 2 == 0 else -1
            pairs.append((core * size + i, core * size + (i + step) % size))
    return lax.ppermute(block, ("core", axis), pairs)


def dot(a, b, dims):
    return lax.dot_general(a, b, (dims, ((), ())), preferred_element_type=F32)


def line_of_4(mine, axis):
    first = jnp.stack([mine, exchange(mine, axis, 4, 0)])
    return [((0, 1), first), ((-1, -2), exchange(first, axis, 4, 1))]


def line_of_8(mine, axis):
    first = jnp.stack([mine, exchange(mine, axis, 8, 0)])
    second = exchange(first, axis, 8, 1)
    third = exchange(second, axis, 8, 0)
    fourth = exchange(third, axis, 8, 1)
    return [((0, 1), first), ((-1, -2), second), ((2, 3), third), ((-3, -4), fourth)]


def place(pairs, at, size, sign):
    block = pairs[0][1]
    whole = jnp.zeros((size, *block.shape[1:]), block.dtype)
    for steps, pair in pairs:
        for i, k in enumerate(steps):
            start = ((at + k * sign) & (size - 1),) + (0,) * (block.ndim - 1)
            whole = lax.dynamic_update_slice(whole, pair[i : i + 1], start)
    return whole


def products(pairs, weight_t, tokens_of, at, size, sign, total):
    shares = []
    for steps, pair in pairs:
        flat = pair.reshape(-1, 1536)
        share = dot(flat, weight_t, ((1,), (0,)))
        shares.append((steps, share.reshape(*pair.shape[:-1], 384)))
        tokens = [
            lax.dynamic_index_in_dim(tokens_of, (at + k * sign) & (size - 1), 0, False)
            for k in steps
        ]
        total = total + dot(flat, jnp.concatenate(tokens, axis=0), ((0,), (0,)))
    return shares, total


def on_device(inputs, pre_act, grad_act, weight_t):
    z, core, x, y = (lax.axis_index(a) for a in ALL)
    hidden = (grad_act.astype(F32) * gelu_prime(pre_act.astype(F32))).astype(BF)
    h = y % 2
    q = x // 2
    same = lax.dynamic_slice_in_dim(hidden, h * 64, 64, 0)
    other = lax.dynamic_slice_in_dim(hidden, (1 - h) * 64, 64, 0)
    same = lax.ppermute(same, ALL, to_slots(0))
    other = lax.ppermute(other, ALL, to_slots(1))
    low = jnp.where(q == 0, same, other)
    high = jnp.where(q == 0, other, same)
    slot = jnp.concatenate([low, high], axis=1)
    part_a, part_b = slot[:PART], slot[PART:]

    all_inputs = lax.all_gather(inputs, ROW, axis=0)
    seen = all_inputs.reshape(2, 4, 2, 2, 2, PART, 384)
    in_a = seen[:, :, :, :, 0].transpose(3, 0, 2, 1, 4, 5).reshape(4, 8 * PART, 384)
    in_b = seen[:, :, :, :, 1].transpose(2, 1, 3, 0, 4, 5).reshape(8, 4 * PART, 384)

    sign_x = 1 - 2 * ((x + core) & 1)
    sign_y = 1 - 2 * ((y + core) & 1)
    lines_b = place(line_of_4(part_b, "x"), x, 4, sign_x)
    lines_a = place(line_of_8(part_a, "y"), y, 8, sign_y)
    pairs_a = line_of_4(lines_a, "x")
    pairs_b = line_of_8(lines_b, "y")
    shares_a, total = products(pairs_a, weight_t, in_a, x, 4, sign_x, 0.0)
    shares_b, total = products(pairs_b, weight_t, in_b, y, 8, sign_y, total)
    grad_weight = total.astype(BF)

    share_a = place(shares_a, x, 4, sign_x).reshape(2, 2, 2, 4, PART, 384)
    share_b = place(shares_b, y, 8, sign_y).reshape(2, 4, 2, 2, PART, 384).transpose(2, 3, 0, 1, 4, 5)
    share = jnp.stack([share_a, share_b], axis=4)
    keep = lax.dynamic_index_in_dim(share, core, 2, False)
    give = lax.dynamic_index_in_dim(share, 1 - core, 2, False).astype(BF)
    both = keep + lax.ppermute(give, "core", [(0, 1), (1, 0)]).astype(F32)
    sent = both.astype(BF).transpose(1, 2, 0, 3, 4, 5).reshape(8, 128, 384)
    parts = lax.all_to_all(sent, "z", 0, 0)
    grad_inputs = parts.astype(F32).sum(axis=0).astype(BF)
    return (grad_inputs, grad_weight)


def solution(mesh):
    fine = Mesh(mesh.devices.reshape(8, 2, 4, 8), ALL)
    placed = P(ROW, COL)
    return jax.shard_map(
        on_device,
        mesh=fine,
        in_specs=(placed,) * 4,
        out_specs=(placed, placed),
        check_vma=False,
    )
```

```python
import jax
import jax.numpy as jnp
from jax import lax
from jax.sharding import Mesh, PartitionSpec as P

ROW = ("z", "core")
COL = ("x", "y")
ALL = ROW + COL
BF, F32 = jnp.bfloat16, jnp.float32
A, B = 24, 40


def gelu_prime(value):
    inner = 0.7978845608 * (value + 0.044715 * value * value * value)
    tanh_val = jnp.tanh(inner)
    slope = 0.7978845608 * (1.0 + 0.134145 * value * value)
    return 0.5 * (1.0 + tanh_val) + 0.5 * value * (1.0 - tanh_val * tanh_val) * slope


def slot_of(row, q):
    z, core = row // 2, row % 2
    x, y = q * 2 + z // 4, core * 4 + z % 4
    return x * 8 + y


def to_slots(swap):
    pairs = []
    for row in range(16):
        for col in range(32):
            q = (col % 2) ^ swap
            pairs.append((row * 32 + col, (col // 2) * 32 + slot_of(row, q)))
    return pairs


def exchange(block, axis, size, turn):
    pairs = []
    for core in range(2):
        for i in range(size):
            step = 1 if (i + core + turn) % 2 == 0 else -1
            j = (i + step) % size
            if axis == "z":
                pairs.append((i * 2 + core, j * 2 + core))
            else:
                pairs.append((core * size + i, core * size + j))
    return lax.ppermute(block, ROW if axis == "z" else ("core", axis), pairs)


def dot(a, b, dims):
    return lax.dot_general(a, b, (dims, ((), ())), preferred_element_type=F32)


def place(pairs, at, size, sign):
    block = pairs[0][1]
    whole = jnp.zeros((size, *block.shape[1:]), block.dtype)
    for steps, pair in pairs:
        for i, k in enumerate(steps):
            start = ((at + k * sign) & (size - 1),) + (0,) * (block.ndim - 1)
            whole = lax.dynamic_update_slice(whole, pair[i : i + 1], start)
    return whole


def products(pairs, weight_t, tokens_of, at, size, sign, total):
    shares = []
    for steps, pair in pairs:
        flat = pair.reshape(-1, 1536)
        share = dot(flat, weight_t, ((1,), (0,)))
        shares.append((steps, share.reshape(*pair.shape[:-1], 384)))
        tokens = [
            lax.dynamic_index_in_dim(tokens_of, (at + k * sign) & (size - 1), 0, False)
            for k in steps
        ]
        total = total + dot(flat, jnp.concatenate(tokens, axis=0), ((0,), (0,)))
    return shares, total


def on_device(inputs, pre_act, grad_act, weight_t):
    z, core, x, y = (lax.axis_index(a) for a in ALL)
    hidden = (grad_act.astype(F32) * gelu_prime(pre_act.astype(F32))).astype(BF)
    h = y % 2
    q = x // 2
    same = lax.dynamic_slice_in_dim(hidden, h * 64, 64, 0)
    other = lax.dynamic_slice_in_dim(hidden, (1 - h) * 64, 64, 0)
    same = lax.ppermute(same, ALL, to_slots(0))
    other = lax.ppermute(other, ALL, to_slots(1))
    low = jnp.where(q == 0, same, other)
    high = jnp.where(q == 0, other, same)
    slot = jnp.concatenate([low, high], axis=1)
    part_a, part_b = slot[:A], slot[A:]

    all_inputs = lax.all_gather(inputs, ROW, axis=0)
    seen = all_inputs.reshape(2, 4, 2, 2, 64, 384)
    in_a = seen[:, :, :, :, :A].transpose(3, 0, 2, 1, 4, 5).reshape(4, 8 * A, 384)
    in_b = seen[:, :, :, :, A:].transpose(2, 1, 3, 0, 4, 5).reshape(8, 4 * B, 384)

    sign_x = 1 - 2 * ((x + core) & 1)
    sign_y = 1 - 2 * ((y + core) & 1)
    a1, b1 = exchange(part_a, "y", 8, 0), exchange(part_b, "x", 4, 0)
    a01, b01 = jnp.stack([part_a, a1]), jnp.stack([part_b, b1])
    a12, b12 = exchange(a01, "y", 8, 1), exchange(b01, "x", 4, 1)
    line_b = place([((0, 1), b01), ((-1, -2), b12)], x, 4, sign_x).reshape(4 * B, 1536)
    third = exchange(jnp.concatenate([a12.reshape(2 * A, 1536), line_b]), "y", 8, 0)
    a23, near_b = third[: 2 * A], third[2 * A :]
    fourth = exchange(jnp.concatenate([third, line_b]), "y", 8, 1)
    a34, pair_b = fourth[: 2 * A], fourth[2 * A :]
    far_b = exchange(pair_b, "y", 8, 0)
    line_a = place(
        [
            ((0, 1), a01),
            ((-1, -2), a12),
            ((2, 3), a23.reshape(2, A, 1536)),
            ((-3, -4), a34.reshape(2, A, 1536)),
        ],
        y,
        8,
        sign_y,
    )
    pair_a = jnp.stack([line_a, exchange(line_a, "x", 4, 0)])
    pairs_a = [((0, 1), pair_a), ((-1, -2), exchange(pair_a, "x", 4, 1))]
    pairs_b = [
        ((0, 1), jnp.concatenate([line_b, near_b]).reshape(2, 4, B, 1536)),
        ((-2, -1), pair_b.reshape(2, 4, B, 1536)),
        ((3, 2), far_b.reshape(2, 4, B, 1536)),
        ((-4, -3), exchange(far_b, "y", 8, 1).reshape(2, 4, B, 1536)),
    ]
    shares_a, total = products(pairs_a, weight_t, in_a, x, 4, sign_x, 0.0)
    shares_b, total = products(pairs_b, weight_t, in_b, y, 8, sign_y, total)
    grad_weight = total.astype(BF)

    share_a = place(shares_a, x, 4, sign_x).reshape(2, 2, 2, 4, A, 384)
    share_b = place(shares_b, y, 8, sign_y).reshape(2, 4, 2, 2, B, 384).transpose(2, 3, 0, 1, 4, 5)
    share = jnp.concatenate([share_a, share_b], axis=4)
    keep = lax.dynamic_index_in_dim(share, core, 2, False)
    give = lax.dynamic_index_in_dim(share, 1 - core, 2, False).astype(BF)
    both = keep + lax.ppermute(give, "core", [(0, 1), (1, 0)]).astype(F32)
    both = both.reshape(2, 8, 64, 384)
    sign_z = 1 - 2 * ((z + core) & 1)

    def own(*steps):
        return jnp.stack(
            [lax.dynamic_index_in_dim(both, (z + k * sign_z) & 7, 1, False) for k in steps]
        )

    sums = own(2, 3) + exchange(own(-3, -4).astype(BF), "z", 8, 1).astype(F32)
    sums = own(-1, -2) + exchange(sums.astype(BF), "z", 8, 0).astype(F32)
    sums = own(0, 1) + exchange(sums.astype(BF), "z", 8, 1).astype(F32)
    sums = sums[0] + exchange(sums[1], "z", 8, 0)
    grad_inputs = sums.reshape(128, 384).astype(BF)
    return (grad_inputs, grad_weight)


def solution(mesh):
    fine = Mesh(mesh.devices.reshape(8, 2, 4, 8), ALL)
    placed = P(ROW, COL)
    return jax.shard_map(
        on_device,
        mesh=fine,
        in_specs=(placed,) * 4,
        out_specs=(placed, placed),
        check_vma=False,
    )
```

```python
import jax
import jax.numpy as jnp
from jax import lax
from jax.sharding import Mesh, PartitionSpec as P

ROW = ("z", "core")
COL = ("x", "y")
ALL = ROW + COL
BF, F32 = jnp.bfloat16, jnp.float32
A, B = 40, 24


def gelu_prime(value):
    inner = 0.7978845608 * (value + 0.044715 * value * value * value)
    tanh_val = jnp.tanh(inner)
    slope = 0.7978845608 * (1.0 + 0.134145 * value * value)
    return 0.5 * (1.0 + tanh_val) + 0.5 * value * (1.0 - tanh_val * tanh_val) * slope


def slot_of(row, q):
    z, core = row // 2, row % 2
    x, y = q * 2 + z // 4, core * 4 + z % 4
    return x * 8 + y


def to_slots(swap):
    pairs = []
    for row in range(16):
        for col in range(32):
            q = (col % 2) ^ swap
            pairs.append((row * 32 + col, (col // 2) * 32 + slot_of(row, q)))
    return pairs


def exchange(block, axis, size, turn):
    pairs = []
    for core in range(2):
        for i in range(size):
            step = 1 if (i + core + turn) % 2 == 0 else -1
            j = (i + step) % size
            if axis == "z":
                pairs.append((i * 2 + core, j * 2 + core))
            else:
                pairs.append((core * size + i, core * size + j))
    return lax.ppermute(block, ROW if axis == "z" else ("core", axis), pairs)


def dot(a, b, dims):
    return lax.dot_general(a, b, (dims, ((), ())), preferred_element_type=F32)


def line_of_4(mine, axis):
    first = jnp.stack([mine, exchange(mine, axis, 4, 0)])
    return [((0, 1), first), ((-1, -2), exchange(first, axis, 4, 1))]


def line_of_8(mine, axis):
    first = jnp.stack([mine, exchange(mine, axis, 8, 0)])
    second = exchange(first, axis, 8, 1)
    third = exchange(second, axis, 8, 0)
    fourth = exchange(third, axis, 8, 1)
    return [((0, 1), first), ((-1, -2), second), ((2, 3), third), ((-3, -4), fourth)]


def place(pairs, at, size, sign):
    block = pairs[0][1]
    whole = jnp.zeros((size, *block.shape[1:]), block.dtype)
    for steps, pair in pairs:
        for i, k in enumerate(steps):
            start = ((at + k * sign) & (size - 1),) + (0,) * (block.ndim - 1)
            whole = lax.dynamic_update_slice(whole, pair[i : i + 1], start)
    return whole


def products(pairs, weight_t, tokens_of, at, size, sign, total):
    shares = []
    for steps, pair in pairs:
        flat = pair.reshape(-1, 1536)
        share = dot(flat, weight_t, ((1,), (0,)))
        shares.append((steps, share.reshape(*pair.shape[:-1], 384)))
        tokens = [
            lax.dynamic_index_in_dim(tokens_of, (at + k * sign) & (size - 1), 0, False)
            for k in steps
        ]
        total = total + dot(flat, jnp.concatenate(tokens, axis=0), ((0,), (0,)))
    return shares, total


def on_device(inputs, pre_act, grad_act, weight_t):
    z, core, x, y = (lax.axis_index(a) for a in ALL)
    hidden = (grad_act.astype(F32) * gelu_prime(pre_act.astype(F32))).astype(BF)
    h = y % 2
    q = x // 2
    same = lax.dynamic_slice_in_dim(hidden, h * 64, 64, 0)
    other = lax.dynamic_slice_in_dim(hidden, (1 - h) * 64, 64, 0)
    same = lax.ppermute(same, ALL, to_slots(0))
    other = lax.ppermute(other, ALL, to_slots(1))
    low = jnp.where(q == 0, same, other)
    high = jnp.where(q == 0, other, same)
    slot = jnp.concatenate([low, high], axis=1)
    part_a, part_b = slot[:A], slot[A:]

    own_z = place(line_of_8(inputs, "z"), z, 8, 1 - 2 * ((z + core) & 1))
    mate_z = lax.ppermute(own_z, "core", [(0, 1), (1, 0)])
    all_inputs = jnp.stack(
        [jnp.where(core == 0, own_z, mate_z), jnp.where(core == 0, mate_z, own_z)], axis=1
    )
    seen = all_inputs.reshape(2, 4, 2, 2, 64, 384)
    in_a = seen[:, :, :, :, :A].transpose(3, 0, 2, 1, 4, 5).reshape(4, 8 * A, 384)
    in_b = seen[:, :, :, :, A:].transpose(2, 1, 3, 0, 4, 5).reshape(8, 4 * B, 384)

    sign_x = 1 - 2 * ((x + core) & 1)
    sign_y = 1 - 2 * ((y + core) & 1)
    lines_b = place(line_of_4(part_b, "x"), x, 4, sign_x)
    lines_a = place(line_of_8(part_a, "y"), y, 8, sign_y)
    pairs_a = line_of_4(lines_a, "x")
    pairs_b = line_of_8(lines_b, "y")
    shares_a, total = products(pairs_a, weight_t, in_a, x, 4, sign_x, 0.0)
    shares_b, total = products(pairs_b, weight_t, in_b, y, 8, sign_y, total)
    grad_weight = total.astype(BF)

    share_a = place(shares_a, x, 4, sign_x).reshape(2, 2, 2, 4, A, 384)
    share_b = place(shares_b, y, 8, sign_y).reshape(2, 4, 2, 2, B, 384).transpose(2, 3, 0, 1, 4, 5)
    share = jnp.concatenate([share_a, share_b], axis=4)
    keep = lax.dynamic_index_in_dim(share, core, 2, False)
    give = lax.dynamic_index_in_dim(share, 1 - core, 2, False).astype(BF)
    both = keep + lax.ppermute(give, "core", [(0, 1), (1, 0)]).astype(F32)
    sent = both.astype(BF).transpose(1, 2, 0, 3, 4).reshape(8, 128, 384)
    parts = lax.all_to_all(sent, "z", 0, 0)
    grad_inputs = parts.astype(F32).sum(axis=0).astype(BF)
    return (grad_inputs, grad_weight)


def solution(mesh):
    fine = Mesh(mesh.devices.reshape(8, 2, 4, 8), ALL)
    placed = P(ROW, COL)
    return jax.shard_map(
        on_device,
        mesh=fine,
        in_specs=(placed,) * 4,
        out_specs=(placed, placed),
        check_vma=False,
    )
```

```python
import jax
import jax.numpy as jnp
from jax import lax
from jax.sharding import Mesh, PartitionSpec as P

ROW = ("z", "core")
COL = ("x", "y")
ALL = ROW + COL
BF, F32 = jnp.bfloat16, jnp.float32
A, B = 40, 24


def gelu_prime(value):
    inner = 0.7978845608 * (value + 0.044715 * value * value * value)
    tanh_val = jnp.tanh(inner)
    slope = 0.7978845608 * (1.0 + 0.134145 * value * value)
    return 0.5 * (1.0 + tanh_val) + 0.5 * value * (1.0 - tanh_val * tanh_val) * slope


def slot_of(row, q):
    z, core = row // 2, row % 2
    x, y = q * 2 + z // 4, core * 4 + z % 4
    return x * 8 + y


def to_slots(swap):
    pairs = []
    for row in range(16):
        for col in range(32):
            q = (col % 2) ^ swap
            pairs.append((row * 32 + col, (col // 2) * 32 + slot_of(row, q)))
    return pairs


def exchange(block, axis, size, turn):
    pairs = []
    for core in range(2):
        for i in range(size):
            step = 1 if (i + core + turn) % 2 == 0 else -1
            j = (i + step) % size
            if axis == "z":
                pairs.append((i * 2 + core, j * 2 + core))
            else:
                pairs.append((core * size + i, core * size + j))
    return lax.ppermute(block, ROW if axis == "z" else ("core", axis), pairs)


def dot(a, b, dims):
    return lax.dot_general(a, b, (dims, ((), ())), preferred_element_type=F32)


def line_of_4(mine, axis):
    first = jnp.stack([mine, exchange(mine, axis, 4, 0)])
    return [((0, 1), first), ((-1, -2), exchange(first, axis, 4, 1))]


def line_of_8(mine, axis):
    first = jnp.stack([mine, exchange(mine, axis, 8, 0)])
    second = exchange(first, axis, 8, 1)
    third = exchange(second, axis, 8, 0)
    fourth = exchange(third, axis, 8, 1)
    return [((0, 1), first), ((-1, -2), second), ((2, 3), third), ((-3, -4), fourth)]


def place(pairs, at, size, sign):
    block = pairs[0][1]
    whole = jnp.zeros((size, *block.shape[1:]), block.dtype)
    for steps, pair in pairs:
        for i, k in enumerate(steps):
            start = ((at + k * sign) & (size - 1),) + (0,) * (block.ndim - 1)
            whole = lax.dynamic_update_slice(whole, pair[i : i + 1], start)
    return whole


def products(pairs, weight_t, tokens_of, at, size, sign, total):
    shares = []
    for steps, pair in pairs:
        flat = pair.reshape(-1, 1536)
        share = dot(flat, weight_t, ((1,), (0,)))
        shares.append((steps, share.reshape(*pair.shape[:-1], 384)))
        tokens = [
            lax.dynamic_index_in_dim(tokens_of, (at + k * sign) & (size - 1), 0, False)
            for k in steps
        ]
        total = total + dot(flat, jnp.concatenate(tokens, axis=0), ((0,), (0,)))
    return shares, total


def on_device(inputs, pre_act, grad_act, weight_t):
    z, core, x, y = (lax.axis_index(a) for a in ALL)
    hidden = (grad_act.astype(F32) * gelu_prime(pre_act.astype(F32))).astype(BF)
    h = y % 2
    q = x // 2
    same = lax.dynamic_slice_in_dim(hidden, h * 64, 64, 0)
    other = lax.dynamic_slice_in_dim(hidden, (1 - h) * 64, 64, 0)
    same = lax.ppermute(same, ALL, to_slots(0))
    other = lax.ppermute(other, ALL, to_slots(1))
    low = jnp.where(q == 0, same, other)
    high = jnp.where(q == 0, other, same)
    slot = jnp.concatenate([low, high], axis=1)
    part_a, part_b = slot[:A], slot[A:]

    in_1 = jnp.stack([inputs, exchange(inputs, "z", 8, 0)])
    in_2 = exchange(in_1, "z", 8, 1)

    sign_x = 1 - 2 * ((x + core) & 1)
    sign_y = 1 - 2 * ((y + core) & 1)
    lines_b = place(line_of_4(part_b, "x"), x, 4, sign_x)
    lines_a = place(line_of_8(part_a, "y"), y, 8, sign_y)
    near = exchange(lines_a, "x", 4, 0)
    back = exchange(lines_a, "x", 4, 1)
    far = exchange(near, "x", 4, 1)
    pairs_a = [((0,), lines_a[None]), ((1,), near[None]), ((-1,), back[None]), ((-2,), far[None])]
    pairs_b = line_of_8(lines_b, "y")
    in_2, held = lax.optimization_barrier((in_2, pairs_b[2][1]))
    pairs_b[2] = (pairs_b[2][0], held)
    in_3 = exchange(in_2, "z", 8, 0)
    in_4 = exchange(in_3, "z", 8, 1)
    own_z = place(
        [((0, 1), in_1), ((-1, -2), in_2), ((2, 3), in_3), ((-3, -4), in_4)],
        z,
        8,
        1 - 2 * ((z + core) & 1),
    )
    mate_z = lax.ppermute(own_z, "core", [(0, 1), (1, 0)])
    all_inputs = jnp.stack(
        [jnp.where(core == 0, own_z, mate_z), jnp.where(core == 0, mate_z, own_z)], axis=1
    )
    seen = all_inputs.reshape(2, 4, 2, 2, 64, 384)
    in_a = seen[:, :, :, :, :A].transpose(3, 0, 2, 1, 4, 5).reshape(4, 8 * A, 384)
    in_b = seen[:, :, :, :, A:].transpose(2, 1, 3, 0, 4, 5).reshape(8, 4 * B, 384)

    shares_a, total = products(pairs_a, weight_t, in_a, x, 4, sign_x, 0.0)
    shares_b, total = products(pairs_b, weight_t, in_b, y, 8, sign_y, total)
    grad_weight = total.astype(BF)

    share_a = place(shares_a, x, 4, sign_x).reshape(2, 2, 2, 4, A, 384)
    share_b = place(shares_b, y, 8, sign_y).reshape(2, 4, 2, 2, B, 384).transpose(2, 3, 0, 1, 4, 5)
    share = jnp.concatenate([share_a, share_b], axis=4)
    keep = lax.dynamic_index_in_dim(share, core, 2, False)
    give = lax.dynamic_index_in_dim(share, 1 - core, 2, False).astype(BF)
    both = keep + lax.ppermute(give, "core", [(0, 1), (1, 0)]).astype(F32)
    sent = both.astype(BF).transpose(1, 2, 0, 3, 4).reshape(8, 128, 384)
    parts = lax.all_to_all(sent, "z", 0, 0)
    grad_inputs = parts.astype(F32).sum(axis=0).astype(BF)
    return (grad_inputs, grad_weight)


def solution(mesh):
    fine = Mesh(mesh.devices.reshape(8, 2, 4, 8), ALL)
    placed = P(ROW, COL)
    return jax.shard_map(
        on_device,
        mesh=fine,
        in_specs=(placed,) * 4,
        out_specs=(placed, placed),
        check_vma=False,
    )
```

```python
import jax
import jax.numpy as jnp
from jax import lax
from jax.sharding import Mesh, PartitionSpec as P

ROW = ("z", "core")
COL = ("x", "y")
ALL = ROW + COL
BF, F32 = jnp.bfloat16, jnp.float32
A, B = 40, 24


def gelu_prime(value):
    inner = 0.7978845608 * (value + 0.044715 * value * value * value)
    tanh_val = jnp.tanh(inner)
    slope = 0.7978845608 * (1.0 + 0.134145 * value * value)
    return 0.5 * (1.0 + tanh_val) + 0.5 * value * (1.0 - tanh_val * tanh_val) * slope


def slot_of(row, q):
    z, core = row // 2, row % 2
    x, y = q * 2 + z // 4, core * 4 + z % 4
    return x * 8 + y


def to_slots(swap):
    pairs = []
    for row in range(16):
        for col in range(32):
            q = (col % 2) ^ swap
            pairs.append((row * 32 + col, (col // 2) * 32 + slot_of(row, q)))
    return pairs


def exchange(block, axis, size, turn):
    pairs = []
    for core in range(2):
        for i in range(size):
            step = 1 if (i + core + turn) % 2 == 0 else -1
            j = (i + step) % size
            if axis == "z":
                pairs.append((i * 2 + core, j * 2 + core))
            else:
                pairs.append((core * size + i, core * size + j))
    return lax.ppermute(block, ROW if axis == "z" else ("core", axis), pairs)


def dot(a, b, dims):
    return lax.dot_general(a, b, (dims, ((), ())), preferred_element_type=F32)


def line_of_4(mine, axis):
    first = jnp.stack([mine, exchange(mine, axis, 4, 0)])
    return [((0, 1), first), ((-1, -2), exchange(first, axis, 4, 1))]


def line_of_8(mine, axis):
    first = jnp.stack([mine, exchange(mine, axis, 8, 0)])
    second = exchange(first, axis, 8, 1)
    third = exchange(second, axis, 8, 0)
    fourth = exchange(third, axis, 8, 1)
    return [((0, 1), first), ((-1, -2), second), ((2, 3), third), ((-3, -4), fourth)]


def place(pairs, at, size, sign):
    block = pairs[0][1]
    whole = jnp.zeros((size, *block.shape[1:]), block.dtype)
    for steps, pair in pairs:
        for i, k in enumerate(steps):
            start = ((at + k * sign) & (size - 1),) + (0,) * (block.ndim - 1)
            whole = lax.dynamic_update_slice(whole, pair[i : i + 1], start)
    return whole


def shares_of(pairs, weight_t):
    shares = []
    for steps, pair in pairs:
        share = dot(pair.reshape(-1, 1536), weight_t, ((1,), (0,)))
        shares.append((steps, share.reshape(*pair.shape[:-1], 384)))
    return shares


def weight_sums(pairs, tokens_of, at, size, sign, total):
    for steps, pair in pairs:
        tokens = [
            lax.dynamic_index_in_dim(tokens_of, (at + k * sign) & (size - 1), 0, False)
            for k in steps
        ]
        flat = pair.reshape(-1, 1536)
        total = total + dot(flat, jnp.concatenate(tokens, axis=0), ((0,), (0,)))
    return total


def on_device(inputs, pre_act, grad_act, weight_t):
    z, core, x, y = (lax.axis_index(a) for a in ALL)
    hidden = (grad_act.astype(F32) * gelu_prime(pre_act.astype(F32))).astype(BF)
    h = y % 2
    q = x // 2
    same = lax.dynamic_slice_in_dim(hidden, h * 64, 64, 0)
    other = lax.dynamic_slice_in_dim(hidden, (1 - h) * 64, 64, 0)
    same = lax.ppermute(same, ALL, to_slots(0))
    other = lax.ppermute(other, ALL, to_slots(1))
    low = jnp.where(q == 0, same, other)
    high = jnp.where(q == 0, other, same)
    slot = jnp.concatenate([low, high], axis=1)
    part_a, part_b = slot[:A], slot[A:]

    in_1 = jnp.stack([inputs, exchange(inputs, "z", 8, 0)])
    in_2 = exchange(in_1, "z", 8, 1)

    sign_x = 1 - 2 * ((x + core) & 1)
    sign_y = 1 - 2 * ((y + core) & 1)
    lines_b = place(line_of_4(part_b, "x"), x, 4, sign_x)
    lines_a = place(line_of_8(part_a, "y"), y, 8, sign_y)
    near = exchange(lines_a, "x", 4, 0)
    back = exchange(lines_a, "x", 4, 1)
    far = exchange(near, "x", 4, 1)
    pairs_a = [((0,), lines_a[None]), ((1,), near[None]), ((-1,), back[None]), ((-2,), far[None])]
    pairs_b = line_of_8(lines_b, "y")
    in_2, held = lax.optimization_barrier((in_2, pairs_b[2][1]))
    pairs_b[2] = (pairs_b[2][0], held)
    in_3 = exchange(in_2, "z", 8, 0)
    in_4 = exchange(in_3, "z", 8, 1)
    own_z = place(
        [((0, 1), in_1), ((-1, -2), in_2), ((2, 3), in_3), ((-3, -4), in_4)],
        z,
        8,
        1 - 2 * ((z + core) & 1),
    )
    mate_z = lax.ppermute(own_z, "core", [(0, 1), (1, 0)])
    all_inputs = jnp.stack(
        [jnp.where(core == 0, own_z, mate_z), jnp.where(core == 0, mate_z, own_z)], axis=1
    )
    seen = all_inputs.reshape(2, 4, 2, 2, 64, 384)
    in_a = seen[:, :, :, :, :A].transpose(3, 0, 2, 1, 4, 5).reshape(4, 8 * A, 384)
    in_b = seen[:, :, :, :, A:].transpose(2, 1, 3, 0, 4, 5).reshape(8, 4 * B, 384)

    shares_a = shares_of(pairs_a, weight_t)
    shares_b = shares_of(pairs_b, weight_t)

    share_a = place(shares_a, x, 4, sign_x).reshape(2, 2, 2, 4, A, 384)
    share_b = place(shares_b, y, 8, sign_y).reshape(2, 4, 2, 2, B, 384).transpose(2, 3, 0, 1, 4, 5)
    share = jnp.concatenate([share_a, share_b], axis=4)
    keep = lax.dynamic_index_in_dim(share, core, 2, False)
    give = lax.dynamic_index_in_dim(share, 1 - core, 2, False).astype(BF)
    mate = lax.ppermute(give, "core", [(0, 1), (1, 0)])
    in_a, in_b, mate = lax.optimization_barrier((in_a, in_b, mate))
    total = weight_sums(pairs_a, in_a, x, 4, sign_x, 0.0)
    total = weight_sums(pairs_b, in_b, y, 8, sign_y, total)
    grad_weight = total.astype(BF)
    both = keep + mate.astype(F32)
    sent = both.astype(BF).transpose(1, 2, 0, 3, 4).reshape(8, 128, 384)
    parts = lax.all_to_all(sent, "z", 0, 0)
    grad_inputs = parts.astype(F32).sum(axis=0).astype(BF)
    return (grad_inputs, grad_weight)


def solution(mesh):
    fine = Mesh(mesh.devices.reshape(8, 2, 4, 8), ALL)
    placed = P(ROW, COL)
    return jax.shard_map(
        on_device,
        mesh=fine,
        in_specs=(placed,) * 4,
        out_specs=(placed, placed),
        check_vma=False,
    )
```

```python
import jax
import jax.numpy as jnp
from jax import lax
from jax.sharding import Mesh, PartitionSpec as P

ROW = ("z", "core")
COL = ("x", "y")
ALL = ROW + COL
BF, F32 = jnp.bfloat16, jnp.float32
A, B = 40, 24


def gelu_prime(value):
    inner = 0.7978845608 * (value + 0.044715 * value * value * value)
    tanh_val = jnp.tanh(inner)
    slope = 0.7978845608 * (1.0 + 0.134145 * value * value)
    return 0.5 * (1.0 + tanh_val) + 0.5 * value * (1.0 - tanh_val * tanh_val) * slope


def slot_of(row, q):
    z, core = row // 2, row % 2
    x, y = z // 2, core * 4 + z % 2 * 2 + q
    return x * 8 + y


def to_slots(swap):
    pairs = []
    for row in range(16):
        for col in range(32):
            q = (col % 2) ^ swap
            pairs.append((row * 32 + col, (col // 2) * 32 + slot_of(row, q)))
    return pairs


def exchange(block, axis, size, turn):
    pairs = []
    for core in range(2):
        for i in range(size):
            step = 1 if (i + core + turn) % 2 == 0 else -1
            j = (i + step) % size
            if axis == "z":
                pairs.append((i * 2 + core, j * 2 + core))
            else:
                pairs.append((core * size + i, core * size + j))
    return lax.ppermute(block, ROW if axis == "z" else ("core", axis), pairs)


def dot(a, b, dims):
    return lax.dot_general(a, b, (dims, ((), ())), preferred_element_type=F32)


def line_of_4(mine, axis):
    first = jnp.stack([mine, exchange(mine, axis, 4, 0)])
    return [((0, 1), first), ((-1, -2), exchange(first, axis, 4, 1))]


def line_of_8(mine, axis):
    first = jnp.stack([mine, exchange(mine, axis, 8, 0)])
    second = exchange(first, axis, 8, 1)
    third = exchange(second, axis, 8, 0)
    fourth = exchange(third, axis, 8, 1)
    return [((0, 1), first), ((-1, -2), second), ((2, 3), third), ((-3, -4), fourth)]


def place(pairs, at, size, sign):
    block = pairs[0][1]
    whole = jnp.zeros((size, *block.shape[1:]), block.dtype)
    for steps, pair in pairs:
        for i, k in enumerate(steps):
            start = ((at + k * sign) & (size - 1),) + (0,) * (block.ndim - 1)
            whole = lax.dynamic_update_slice(whole, pair[i : i + 1], start)
    return whole


def shares_of(pairs, weight_t):
    shares = []
    for steps, pair in pairs:
        share = dot(pair.reshape(-1, 1536), weight_t, ((1,), (0,)))
        shares.append((steps, share.reshape(*pair.shape[:-1], 384)))
    return shares


def weight_sums(pairs, tokens_of, at, size, sign, total):
    for steps, pair in pairs:
        tokens = [
            lax.dynamic_index_in_dim(tokens_of, (at + k * sign) & (size - 1), 0, False)
            for k in steps
        ]
        flat = pair.reshape(-1, 1536)
        total = total + dot(flat, jnp.concatenate(tokens, axis=0), ((0,), (0,)))
    return total


def on_device(inputs, pre_act, grad_act, weight_t):
    z, core, x, y = (lax.axis_index(a) for a in ALL)
    hidden = (grad_act.astype(F32) * gelu_prime(pre_act.astype(F32))).astype(BF)
    h = y % 2
    q = y & 1
    same = lax.dynamic_slice_in_dim(hidden, h * 64, 64, 0)
    other = lax.dynamic_slice_in_dim(hidden, (1 - h) * 64, 64, 0)
    same = lax.ppermute(same, ALL, to_slots(0))
    other = lax.ppermute(other, ALL, to_slots(1))
    low = jnp.where(q == 0, same, other)
    high = jnp.where(q == 0, other, same)
    slot = jnp.concatenate([low, high], axis=1)
    part_a, part_b = slot[:A], slot[A:]

    in_1 = jnp.stack([inputs, exchange(inputs, "z", 8, 0)])
    in_2 = exchange(in_1, "z", 8, 1)

    sign_x = 1 - 2 * ((x + core) & 1)
    sign_y = 1 - 2 * ((y + core) & 1)
    lines_b = place(line_of_4(part_b, "x"), x, 4, sign_x)
    lines_a = place(line_of_8(part_a, "y"), y, 8, sign_y)
    near = exchange(lines_a, "x", 4, 0)
    back = exchange(lines_a, "x", 4, 1)
    far = exchange(near, "x", 4, 1)
    pairs_a = [((0,), lines_a[None]), ((1,), near[None]), ((-1,), back[None]), ((-2,), far[None])]
    pairs_b = line_of_8(lines_b, "y")
    in_2, held = lax.optimization_barrier((in_2, pairs_b[2][1]))
    pairs_b[2] = (pairs_b[2][0], held)
    in_3 = exchange(in_2, "z", 8, 0)
    in_4 = exchange(in_3, "z", 8, 1)
    own_z = place(
        [((0, 1), in_1), ((-1, -2), in_2), ((2, 3), in_3), ((-3, -4), in_4)],
        z,
        8,
        1 - 2 * ((z + core) & 1),
    )
    mate_z = lax.ppermute(own_z, "core", [(0, 1), (1, 0)])
    all_inputs = jnp.stack(
        [jnp.where(core == 0, own_z, mate_z), jnp.where(core == 0, mate_z, own_z)], axis=1
    )
    seen = all_inputs.reshape(4, 2, 2, 2, 64, 384)
    in_a = seen[:, :, :, :, :A].transpose(0, 2, 1, 3, 4, 5).reshape(4, 8 * A, 384)
    in_b = seen[:, :, :, :, A:].transpose(2, 1, 3, 0, 4, 5).reshape(8, 4 * B, 384)

    shares_a = shares_of(pairs_a, weight_t)
    shares_b = shares_of(pairs_b, weight_t)

    share_a = place(shares_a, x, 4, sign_x).reshape(4, 2, 4, A, 384)
    share_b = place(shares_b, y, 8, sign_y).reshape(2, 4, 4, B, 384).transpose(2, 0, 1, 3, 4)
    share = jnp.concatenate([share_a, share_b], axis=3)
    keep = lax.dynamic_index_in_dim(share, core, 1, False)
    give = lax.dynamic_index_in_dim(share, 1 - core, 1, False).astype(BF)
    mate = lax.ppermute(give, "core", [(0, 1), (1, 0)])
    in_a, in_b, mate = lax.optimization_barrier((in_a, in_b, mate))
    total = weight_sums(pairs_a, in_a, x, 4, sign_x, 0.0)
    total = weight_sums(pairs_b, in_b, y, 8, sign_y, total)
    grad_weight = total.astype(BF)
    both = keep + mate.astype(F32)
    sent = both.astype(BF).reshape(8, 128, 384)
    parts = lax.all_to_all(sent, "z", 0, 0)
    grad_inputs = parts.astype(F32).sum(axis=0).astype(BF)
    return (grad_inputs, grad_weight)


def solution(mesh):
    fine = Mesh(mesh.devices.reshape(8, 2, 4, 8), ALL)
    placed = P(ROW, COL)
    return jax.shard_map(
        on_device,
        mesh=fine,
        in_specs=(placed,) * 4,
        out_specs=(placed, placed),
        check_vma=False,
    )
```
